256 devices in a mesh: row: 16 (over x_hi, y, core), col: 16 (over z, x_lo).
Axes of the slice: x: 4 (x_hi: 2, x_lo: 2; x = x_hi * 2 + x_lo), y: 4, z: 8, core: 2. Of those that a mesh axis runs over, the one named last changes fastest.
Arguments:
- counts: int32 [16384, 16384], P('row', 'col'), may hold values from 0 to 400, as said below
- vectors: bfloat16 [16384, 512], P(('col', 'row')), may hold values from -0.59765625 to 0.59765625
- accum: float32 [16384, 512], P(('col', 'row')), may hold values from 0.5 to 4
Outputs:
- updated: bfloat16 [16384, 512], P(('col', 'row'))
- accum_new: float32 [16384, 512], P(('col', 'row'))
The draws below stay inside these ranges and needn't reach their ends.
Inputs may be any that keep to these rules, and one draw needn't show every extreme that they name: Every row and every column holds at least one nonzero count; about a third of the counts are zero.
All inputs are finite; a program needn't handle non-finite values.
Results may differ from the reference program's by a relative error of at most 0.0041.
Values may be sent and summed in bfloat16 or wider, within the bound.
A program may use at most 64 MiB of HBM per device.

```python
import math
import jax
import jax.numpy as jnp
from jax import lax

BLOCK = 1024
DIM = 512
WORDS = 16384
N_ROW = 16


def draw_counts(key, part):
    key = jax.random.fold_in(key, 7)
    key_rows, key_cols, key_raw, key_keep = jax.random.split(key, 4)
    total_words = BLOCK * N_ROW
    index = jnp.arange(total_words, dtype=jnp.int32)
    row_level = jax.random.randint(key_rows, (total_words,), 2, 40) + 40 * index // total_words
    col_level = jax.random.randint(key_cols, (total_words,), 2, 40) + 40 * index // total_words
    ceiling = row_level[:, None] * col_level[None, :] // 8 + 1
    raw = jnp.minimum(jax.random.randint(key_raw, (total_words, total_words), 1, ceiling + 1), 400)
    keep = jax.random.randint(key_keep, (total_words, total_words), 0, 3) > 0
    anchor = (index[:, None] + index[None, :]) % 61 == 0
    result = jnp.where(keep | anchor, raw, 0)
    corner = (index[:, None] == total_words - 1) & (index[None, :] == total_words - 1)
    return jnp.where(corner, 400, result).astype(jnp.int32)


def steps_of(stream_key, extent, shards, smallest, top_value):
    def one(axis_at, shards_of):
        steps = jax.random.uniform(jax.random.fold_in(jax.random.fold_in(stream_key, 6), axis_at), (shards_of,), jnp.float32, smallest / len(shards), top_value / len(shards))
        return jnp.repeat(jnp.exp(steps), extent[axis_at] // shards_of).reshape((-1,) + (1,) * (len(extent) - axis_at - 1))

    loudness = one(*shards[0])
    for cut in shards[1:]:
        loudness = loudness * one(*cut)
    return loudness


def centred(key, extent, scale, most, cuts=(), held_as=jnp.bfloat16):
    level = steps_of(key, extent, cuts, -0.22, 0.18) if cuts else 1.0
    entries = jax.random.normal(key, extent, jnp.float32) * scale * level
    return jnp.minimum(jnp.maximum(entries, -most), most).astype(held_as)


def setup_inputs(seed: int = 0) -> dict:
    streams_of = jax.random.split(jax.random.key(seed), 4)
    return {
        "counts": draw_counts(jax.random.fold_in(streams_of[3], 71), 0),
        "vectors": centred(streams_of[1], (WORDS, DIM), 0.1, 0.59765625, ((0, 256),)),
        "accum": jnp.clip(jnp.exp(math.log(4.0) - 2.0794415 * jax.random.uniform(streams_of[2], (WORDS, DIM), jnp.float32) ** steps_of(streams_of[2], (WORDS, DIM), ((0, 256),), -0.2, 0.2)), 0.5, 4.0),
    }


def reference(counts, vectors, accum):
    total_words = counts.shape[0]
    width = vectors.shape[1]
    block = total_words // N_ROW
    blocks = counts.reshape(N_ROW, block, total_words)

    def margins(carry, piece):
        values = piece.astype(jnp.float32)
        return (carry + lax.optimization_barrier(jnp.sum(values, axis=0)), lax.optimization_barrier(jnp.sum(values, axis=1)))
    col_marg, row_marg = lax.scan(margins, jnp.zeros((total_words,), jnp.float32), blocks)
    row_marg = row_marg.reshape(total_words)
    total = jnp.sum(row_marg)
    log_cols = jnp.log(col_marg)
    log_total = jnp.log(total)

    def sweep(carry, item):
        piece, rows, marg = item
        values = piece.astype(jnp.float32)
        scores = lax.dot_general(rows, vectors, (((1,), (1,)), ((), ())), preferred_element_type=jnp.float32)
        pmi = jnp.log(jnp.maximum(values, 1.0)) + log_total - jnp.log(marg)[:, None] - log_cols[None, :]
        gap = scores - pmi
        weight = 0.1 + 0.25 * jnp.sqrt(values)
        resid = (1.0 / 32.0 * jnp.where(piece > 0, weight * gap, jax.nn.sigmoid(gap))).astype(jnp.bfloat16)
        row_grad = jnp.dot(resid, vectors, preferred_element_type=jnp.float32)
        col_grad = lax.dot_general(resid, rows, (((0,), (0,)), ((), ())), preferred_element_type=jnp.float32)
        return (carry + col_grad, row_grad)
    col_grad, row_grads = lax.scan(sweep, jnp.zeros((total_words, width), jnp.float32), (blocks, vectors.reshape(N_ROW, block, width), row_marg.reshape(N_ROW, block)))
    grad = col_grad + row_grads.reshape(total_words, width)
    accum_new = accum + grad * grad
    updated = (vectors.astype(jnp.float32) - 0.5 * grad / jnp.sqrt(accum_new)).astype(jnp.bfloat16)
    return (updated, accum_new)
```

```python
import functools

import jax
import jax.numpy as jnp
from jax import lax
from jax.experimental import pallas as pl
from jax.experimental.pallas import tpu as pltpu
from jax.sharding import PartitionSpec as P

MESH = pl.DeviceIdType.MESH
F32 = jnp.float32
BF16 = jnp.bfloat16
N = 16
B = 1024
S = 64
D = 512
C = 128
NC = B // C


def rows(i, size):
    return pl.ds(pl.multiple_of(i * size, size), size)


def kernel(
    counts_ref, vec_ref, acc_ref, upd_ref, accn_ref,
    cnt, colv, rowv, logx, weight, resid, score, part, ct, rt,
    rs_mine, cs_mine, tot_mine, rs_all, cs_all, tot_all,
    rsend, csend, rrecv, crecv, tsend, trecv,
    cnt_sem, cv_s, cv_r, tv_s, tv_r, rv_s, rv_r,
    rm_s, rm_r, cm_s, cm_r, tm_s, tm_r,
    rg_s, rg_r, cg_s, cg_r, tg_s, tg_r,
):
    r = lax.axis_index("row")
    c = lax.axis_index("col")
    off_diag = r != c

    def cnt_copy(k):
        return pltpu.make_async_copy(
            counts_ref.at[rows(k, C)], cnt.at[rows(k, C)], cnt_sem.at[k]
        )

    for k in range(NC):
        cnt_copy(k).start()

    barrier = pltpu.get_barrier_semaphore()

    def greet(d, _):
        pl.semaphore_signal(barrier, inc=1, device_id=(lax.rem(r + d, N), c), device_id_type=MESH)
        pl.semaphore_signal(barrier, inc=1, device_id=(r, lax.rem(c + d, N)), device_id_type=MESH)
        return 0

    lax.fori_loop(1, N, greet, 0)

    @pl.when(off_diag)
    def _():
        pl.semaphore_signal(barrier, inc=1, device_id=(c, r), device_id_type=MESH)
        pl.semaphore_wait(barrier, 2 * (N - 1) + 1)

    @pl.when(jnp.logical_not(off_diag))
    def _():
        pl.semaphore_wait(barrier, 2 * (N - 1))

    def remote(src, dst, ssem, rsem, dev):
        return pltpu.make_async_remote_copy(
            src_ref=src, dst_ref=dst, send_sem=ssem, recv_sem=rsem, device_id=dev, device_id_type=MESH
        )

    def spread(axis, src, dst, ssem, rsem):
        me = r if axis == 0 else c

        def one(d, _):
            o = lax.rem(me + d, N)
            dev = (o, c) if axis == 0 else (r, o)
            remote(src(o), dst(me), ssem.at[o], rsem.at[me], dev).start()
            return 0

        lax.fori_loop(1, N, one, 0)

    def collect(axis, src, dst, ssem, rsem, send=True, recv=True):
        me = r if axis == 0 else c

        def one(d, _):
            o = lax.rem(me + d, N)
            dev = (o, c) if axis == 0 else (r, o)
            if recv:
                remote(src(o), dst(o), ssem.at[o], rsem.at[o], dev).wait_recv()
            if send:
                remote(src(o), dst(o), ssem.at[o], rsem.at[o], dev).wait_send()
            return 0

        lax.fori_loop(1, N, one, 0)

    tvec = remote(vec_ref, rowv.at[rows(r, S)], tv_s, tv_r, (c, r))

    @pl.when(off_diag)
    def _():
        tvec.start()

    cv = (0, lambda o: vec_ref, lambda o: colv.at[rows(o, S)], cv_s, cv_r)
    spread(*cv)
    colv[rows(r, S), :] = vec_ref[...]

    @pl.when(jnp.logical_not(off_diag))
    def _():
        rowv[rows(c, S), :] = vec_ref[...]

    @pl.when(off_diag)
    def _():
        tvec.wait_recv()

    rv = (1, lambda o: rowv.at[rows(c, S)], lambda o: rowv.at[rows(o, S)], rv_s, rv_r)
    spread(*rv)

    col8 = jnp.zeros((8, B), F32)
    for k in range(NC):
        cnt_copy(k).wait()

        def strip(i, acc, k=k):
            x = cnt[rows(k * (C // 8) + i, 8), :].astype(F32)
            p = x[:, 0:128]
            for q in range(1, 8):
                p = p + x[:, q * 128 : (q + 1) * 128]
            part[rows(i, 8), :] = p
            return acc + x

        col8 = lax.fori_loop(0, C // 8, strip, col8, unroll=4)
        rs_mine[k : k + 1, :] = jnp.sum(part[...].T, axis=0, keepdims=True)
    col1 = jnp.sum(col8, axis=0, keepdims=True)
    for k in range(8):
        cs_mine[k : k + 1, :] = col1[:, k * 128 : (k + 1) * 128]

    rm = (1, lambda o: rs_mine, lambda o: rs_all.at[o], rm_s, rm_r)
    cm = (0, lambda o: cs_mine, lambda o: cs_all.at[o], cm_s, cm_r)
    spread(*rm)
    spread(*cm)
    rs_all[c] = rs_mine[...]
    cs_all[r] = cs_mine[...]

    def prep(i, _):
        x = cnt[rows(i, 8), :].astype(F32)
        logx[rows(i, 8), :] = jnp.log(jnp.maximum(x, 1.0))
        w = (1.0 / 32.0) * (0.1 + 0.25 * jnp.sqrt(x))
        weight[rows(i, 8), :] = jnp.where(x > 0.0, w, 0.0)
        return 0

    lax.fori_loop(0, B // 8, prep, 0, unroll=2)

    collect(*rm)
    rsum = jnp.sum(rs_all[...], axis=0)
    tot_mine[...] = jnp.full((8, 128), jnp.sum(rsum), F32)
    tm = (0, lambda o: tot_mine, lambda o: tot_all.at[o], tm_s, tm_r)
    spread(*tm)
    tot_all[r] = tot_mine[...]
    rlog = jnp.log(rsum)
    for k in range(NC):
        rt[k * C : (k + 1) * C, :] = jnp.broadcast_to(rlog[k : k + 1, :], (C, 128)).T
    collect(*cm)
    clog = jnp.log(jnp.sum(cs_all[...], axis=0))
    collect(*tm)
    clog = clog - jnp.log(jnp.sum(tot_all[...], axis=0))
    for k in range(8):
        ct[0:1, k * 128 : (k + 1) * 128] = clog[k : k + 1, :]

    collect(*cv)
    collect(*rv)

    def chunk(k, _):
        here = rows(k, C)
        score[...] = lax.dot_general(
            rowv[here, :], colv[...], (((1,), (1,)), ((), ())), preferred_element_type=F32
        )

        def strip(i, _):
            at = rows(k * (C // 16) + i, 16)
            rl = rt[at, :]
            rl = jnp.concatenate([rl] * 8, axis=1)
            gap = score[rows(i, 16), :] - logx[at, :] + (rl + ct[0:1, :])
            w = weight[at, :]
            sig = (1.0 / 32.0) * jax.nn.sigmoid(gap)
            resid[at, :] = jnp.where(w > 0.0, w * gap, sig).astype(BF16)
            return 0

        lax.fori_loop(0, C // 16, strip, 0, unroll=2)
        rsend[here, :] = jnp.dot(resid[here, :], colv[...], preferred_element_type=F32).astype(BF16)
        for h in range(2):
            o = 2 * k + h

            @pl.when(o != c)
            def _():
                remote(
                    rsend.at[rows(o, S)], rrecv.at[c], rg_s.at[o], rg_r.at[c], (r, o)
                ).start()

        return 0

    lax.fori_loop(0, NC, chunk, 0)

    def cchunk(k, _):
        here = rows(k, C)
        csend[here, :] = lax.dot_general(
            resid[:, here], rowv[...], (((0,), (0,)), ((), ())), preferred_element_type=F32
        ).astype(BF16)
        for h in range(2):
            o = 2 * k + h

            @pl.when(o != r)
            def _():
                remote(
                    csend.at[rows(o, S)], crecv.at[r], cg_s.at[o], cg_r.at[r], (o, c)
                ).start()

        return 0

    lax.fori_loop(0, NC, cchunk, 0)

    rg = (1, lambda o: rsend.at[rows(o, S)], lambda o: rrecv.at[o], rg_s, rg_r)
    collect(*rg)
    rrecv[c] = rsend[rows(c, S), :]
    tgrad = remote(tsend, trecv, tg_s, tg_r, (c, r))
    tsend[...] = jnp.sum(rrecv[...].astype(F32), axis=0)

    @pl.when(off_diag)
    def _():
        tgrad.start()

    @pl.when(jnp.logical_not(off_diag))
    def _():
        trecv[...] = tsend[...]

    cg = (0, lambda o: csend.at[rows(o, S)], lambda o: crecv.at[o], cg_s, cg_r)
    collect(*cg)
    crecv[r] = csend[rows(r, S), :]
    grad = jnp.sum(crecv[...].astype(F32), axis=0)

    @pl.when(off_diag)
    def _():
        tvec.wait_send()
        tgrad.wait()

    grad = grad + trecv[...]
    accn = acc_ref[...] + grad * grad
    accn_ref[...] = accn
    upd_ref[...] = (vec_ref[...].astype(F32) - 0.5 * grad / jnp.sqrt(accn)).astype(BF16)


def shards(counts, vectors, accum):
    vmem = pl.BlockSpec(memory_space=pltpu.VMEM)
    dma = pltpu.SemaphoreType.DMA
    many = dma((N,))
    one = dma(())
    return pl.pallas_call(
        kernel,
        out_shape=(
            jax.ShapeDtypeStruct((S, D), BF16),
            jax.ShapeDtypeStruct((S, D), F32),
        ),
        in_specs=[pl.BlockSpec(memory_space=pl.ANY), vmem, vmem],
        out_specs=(vmem, vmem),
        scratch_shapes=[
            pltpu.VMEM((B, B), jnp.int32),
            pltpu.VMEM((B, D), BF16),
            pltpu.VMEM((B, D), BF16),
            pltpu.VMEM((B, B), F32),
            pltpu.VMEM((B, B), F32),
            pltpu.VMEM((B, B), BF16),
            pltpu.VMEM((C, B), F32),
            pltpu.VMEM((C, 128), F32),
            pltpu.VMEM((8, B), F32),
            pltpu.VMEM((B, 128), F32),
            pltpu.VMEM((8, 128), F32),
            pltpu.VMEM((8, 128), F32),
            pltpu.VMEM((8, 128), F32),
            pltpu.VMEM((N, 8, 128), F32),
            pltpu.VMEM((N, 8, 128), F32),
            pltpu.VMEM((N, 8, 128), F32),
            pltpu.VMEM((B, D), BF16),
            pltpu.VMEM((B, D), BF16),
            pltpu.VMEM((N, S, D), BF16),
            pltpu.VMEM((N, S, D), BF16),
            pltpu.VMEM((S, D), F32),
            pltpu.VMEM((S, D), F32),
            dma((NC,)), many, many, one, one, many, many,
            many, many, many, many, many, many,
            many, many, many, many, one, one,
        ],
        compiler_params=pltpu.CompilerParams(
            collective_id=1, has_side_effects=True, vmem_limit_bytes=48 * 2**20
        ),
        name="swivel_step",
    )(counts, vectors, accum)


def solution(mesh):
    return jax.shard_map(
        shards,
        mesh=mesh,
        in_specs=(P("row", "col"), P(("col", "row"), None), P(("col", "row"), None)),
        out_specs=(P(("col", "row"), None), P(("col", "row"), None)),
        check_vma=False,
    )
```

```python
import jax
import jax.numpy as jnp
from jax import lax
from jax.experimental import pallas as pl
from jax.experimental.pallas import tpu as pltpu
from jax.sharding import PartitionSpec as P

MESH = pl.DeviceIdType.MESH
F32 = jnp.float32
BF16 = jnp.bfloat16
N = 16
B = 1024
S = 64
D = 512
C = 128
NC = B // C


def rows(i, size):
    return pl.ds(pl.multiple_of(i * size, size), size)


def kernel(
    counts_ref, vec_ref, acc_ref, upd_ref, accn_ref,
    cnt, colv, rowv, logx, weight, resid, score, part, ct, rt,
    rs_mine, cs_mine, tot_mine, rs_two, cs_two, tot_two, rs_got, cs_got, tot_got, rs_all, cs_all, tot_all,
    rsend, mid, zsend, rrecv, cown, cxs, cxr, csend, crecv,
    cnt_sem, cv_s, cv_r, cf_s, rv_s, rv_r, rf_s,
    pair_s, pair_r, rm_s, rm_r, cm_s, cm_r, tm_s, tm_r,
    md_s, md_r, rg_s, rg_r, cx_s, cx_r, cg_s, cg_r,
):
    r = lax.axis_index("row")
    c = lax.axis_index("col")
    m, core = r // 2, r % 2
    xh, y = m // 4, m % 4
    z, xl = c // 2, c % 2
    r_other = 2 * m + (1 - core)
    c_other = 2 * z + (1 - xl)
    on_diag = r == c

    def remote(src, dst, ssem, rsem, dev):
        return pltpu.make_async_remote_copy(
            src_ref=src, dst_ref=dst, send_sem=ssem, recv_sem=rsem, device_id=dev, device_id_type=MESH
        )

    def near(p):
        return lax.rem(m + p, 8)

    def cnt_copy(k):
        return pltpu.make_async_copy(
            counts_ref.at[rows(k, C)], cnt.at[rows(k, C)], cnt_sem.at[k]
        )

    for k in range(NC):
        cnt_copy(k).start()

    barrier = pltpu.get_barrier_semaphore()

    def hello(dev):
        pl.semaphore_signal(barrier, inc=1, device_id=dev, device_id_type=MESH)

    def greet_plane(d, _):
        o = lax.rem(r + d, N)
        hello((o, c))
        hello((o, c_other))
        return 0

    hello((r, c_other))
    lax.fori_loop(1, N, greet_plane, 0)

    def greet(d, _):
        hello((r, 2 * lax.rem(z + d, 8) + xl))
        return 0

    lax.fori_loop(1, 8, greet, 0)

    def greet_far(i, _):
        @pl.when(jnp.logical_not(jnp.logical_and(on_diag, i == z)))
        def _():
            hello((c, 2 * i + core))
            hello((2 * i + xl, r))

        return 0

    lax.fori_loop(0, 8, greet_far, 0)

    col8 = jnp.zeros((8, B), F32)
    for k in range(NC):
        cnt_copy(k).wait()

        def strip(i, acc, k=k):
            x = cnt[rows(k * (C // 8) + i, 8), :].astype(F32)
            p = x[:, 0:128]
            for q in range(1, 8):
                p = p + x[:, q * 128 : (q + 1) * 128]
            part[rows(i, 8), :] = p
            return acc + x

        col8 = lax.fori_loop(0, C // 8, strip, col8, unroll=4)
        rs_mine[k : k + 1, :] = jnp.sum(part[...].T, axis=0, keepdims=True)
    col1 = jnp.sum(col8, axis=0, keepdims=True)
    for k in range(8):
        cs_mine[k : k + 1, :] = col1[:, k * 128 : (k + 1) * 128]

    @pl.when(on_diag)
    def _():
        pl.semaphore_wait(barrier, 52)

    @pl.when(jnp.logical_not(on_diag))
    def _():
        pl.semaphore_wait(barrier, 54)

    pair_row = remote(rs_mine, rs_got, pair_s.at[0], pair_r.at[0], (r, c_other))
    pair_col = remote(cs_mine, cs_got, pair_s.at[1], pair_r.at[1], (r_other, c))
    pair_tot = remote(tot_mine, tot_got, pair_s.at[2], pair_r.at[2], (r_other, c))

    pair_row.start()
    pair_col.start()

    def rv_copy(i):
        return remote(vec_ref, rowv.at[rows(r, S)], rv_s.at[i], rv_r.at[r], (c, 2 * i + core))

    def rv_start(d, _):
        i = lax.rem(z + d, 8)

        @pl.when(jnp.logical_not(jnp.logical_and(on_diag, i == z)))
        def _():
            rv_copy(i).start()

        return 0

    lax.fori_loop(0, 8, rv_start, 0)

    @pl.when(on_diag)
    def _():
        rowv[rows(r, S), :] = vec_ref[...]

    def rf_copy(i):
        at = rows(2 * i + xl, S)
        return remote(rowv.at[at], rowv.at[at], rf_s.at[i], rv_r.at[2 * i + xl], (r, c_other))

    def rv_forward(p):
        i = near(p)

        @pl.when(jnp.logical_not(jnp.logical_and(on_diag, i == z)))
        def _():
            rf_copy(i).wait_recv()

        rf_copy(i).start()

    def cv_copy(d):
        return remote(
            vec_ref, colv.at[rows(r, S)], cv_s.at[d], cv_r.at[r], (2 * lax.rem(m + d, 8) + core, c)
        )

    cv_core = remote(vec_ref, colv.at[rows(r, S)], cv_s.at[0], cv_r.at[r], (r_other, c))
    for d in range(1, 8):
        cv_copy(d).start()
    cv_core.start()
    colv[rows(r, S), :] = vec_ref[...]

    def cf_copy(d):
        o = 2 * lax.rem(m + d, 8) + core
        block = colv.at[rows(o, S)]
        return remote(block, block, cf_s.at[d], cv_r.at[o], (r_other, c))

    def cv_forward(d):
        cf_copy(d).wait_recv()
        cf_copy(d).start()

    def tile_copy(axis, src, dst, ssem, rsem, o, slot):
        dev = (2 * o + core, c) if axis == 0 else (r, 2 * o + xl)
        return remote(src, dst.at[slot], ssem.at[o], rsem.at[slot], dev)

    def spread(axis, src, dst, ssem, rsem):
        me = m if axis == 0 else z

        def one(d, _):
            tile_copy(axis, src, dst, ssem, rsem, lax.rem(me + d, 8), me).start()
            return 0

        lax.fori_loop(1, 8, one, 0)
        dst[me] = src[...]

    def collect(axis, src, dst, ssem, rsem):
        me = m if axis == 0 else z

        def one(d, _):
            o = lax.rem(me + d, 8)
            tile_copy(axis, src, dst, ssem, rsem, o, o).wait()
            return 0

        lax.fori_loop(1, 8, one, 0)
        return jnp.sum(dst[...], axis=0)

    rm = (1, rs_two, rs_all, rm_s, rm_r)
    cm = (0, cs_two, cs_all, cm_s, cm_r)
    tm = (0, tot_two, tot_all, tm_s, tm_r)

    def prep(i, _):
        x = cnt[rows(i, 8), :].astype(F32)
        logx[rows(i, 8), :] = jnp.log(jnp.maximum(x, 1.0))
        w = (1.0 / 32.0) * (0.1 + 0.25 * jnp.sqrt(x))
        weight[rows(i, 8), :] = jnp.where(x > 0.0, w, 0.0)
        return 0

    def prep_part(k):
        lax.fori_loop(k * 32, (k + 1) * 32, prep, 0, unroll=2)

    cv_forward(1)
    cv_forward(2)
    cv_forward(3)
    pair_row.wait()
    rs_two[...] = rs_mine[...] + rs_got[...]
    spread(*rm)
    pair_col.wait()
    cs_two[...] = cs_mine[...] + cs_got[...]
    spread(*cm)
    rv_forward(0)
    rv_forward(1)
    cv_forward(7)
    cv_forward(6)
    cv_forward(5)
    cv_forward(4)
    rv_forward(2)
    rv_forward(3)
    prep_part(0)
    rsum = collect(*rm)
    tot_mine[...] = jnp.full((8, 128), jnp.sum(rsum), F32)
    pair_tot.start()
    rv_forward(4)
    rv_forward(5)
    prep_part(1)
    pair_tot.wait()
    tot_two[...] = tot_mine[...] + tot_got[...]
    spread(*tm)
    rv_forward(6)
    rv_forward(7)
    prep_part(2)
    prep_part(3)
    rlog = jnp.log(rsum)
    for k in range(NC):
        rt[k * C : (k + 1) * C, :] = jnp.broadcast_to(rlog[k : k + 1, :], (C, 128)).T
    clog = jnp.log(collect(*cm))
    cv_core.wait_send()

    def cv_rest(d, _):
        o = 2 * lax.rem(m + d, 8) + 1 - core
        block = colv.at[rows(o, S)]
        remote(block, block, cf_s.at[0], cv_r.at[o], (r_other, c)).wait_recv()
        return 0

    lax.fori_loop(0, 8, cv_rest, 0)
    clog = clog - jnp.log(collect(*tm))
    for k in range(8):
        ct[0:1, k * 128 : (k + 1) * 128] = clog[k : k + 1, :]

    def md_copy(j):
        return remote(rsend.at[rows(j, S)], mid.at[2 * m + xl], md_s.at[j], md_r.at[2 * m + xl], (j, 2 * z + core))

    stays = core == xl

    def chunk(p):
        n = near(p)
        here = rows(n, C)
        late = 2 * n + 1 - xl
        block = rowv.at[rows(late, S)]
        remote(block, block, rf_s.at[n], rv_r.at[late], (r, c_other)).wait_recv()
        score[...] = lax.dot_general(
            rowv[here, :], colv[...], (((1,), (1,)), ((), ())), preferred_element_type=F32
        )

        def strip(i, _):
            at = rows(n * (C // 16) + i, 16)
            rl = rt[at, :]
            rl = jnp.concatenate([rl] * 8, axis=1)
            gap = score[rows(i, 16), :] - logx[at, :] + (rl + ct[0:1, :])
            w = weight[at, :]
            sig = (1.0 / 64.0) + (1.0 / 64.0) * jnp.tanh(0.5 * gap)
            resid[at, :] = jnp.where(w > 0.0, w * gap, sig).astype(BF16)
            return 0

        lax.fori_loop(0, C // 16, strip, 0, unroll=2)
        out = jnp.dot(resid[here, :], colv[...], preferred_element_type=F32)

        rsend[here, :] = out.astype(BF16)
        for half in range(2):
            mine = jnp.logical_and(stays, 2 * n + half == r)

            @pl.when(jnp.logical_not(mine))
            def _():
                md_copy(2 * n + half).start()

            @pl.when(mine)
            def _():
                mid[2 * m + xl] = rsend[rows(2 * n + half, S), :]

    def rg_copy(n, slot):
        return remote(zsend.at[n], rrecv.at[slot], rg_s.at[n], rg_r.at[slot], (r, 2 * n + xl))

    def reduce(p):
        n = lax.rem(m + 8 - p, 8)
        for half in range(2):
            slot = 2 * n + half

            @pl.when(jnp.logical_not(jnp.logical_and(stays, slot == 2 * m + xl)))
            def _():
                remote(mid.at[slot], mid.at[slot], md_s.at[0], md_r.at[slot], (r_other, c)).wait_recv()

        zsend[n] = (mid[2 * n].astype(F32) + mid[2 * n + 1].astype(F32)).astype(BF16)

        @pl.when(n != z)
        def _():
            rg_copy(n, z).start()

        @pl.when(n == z)
        def _():
            rrecv[z] = zsend[n]

    def cx_copy(n):
        return remote(cxs.at[n], cxr.at[n], cx_s.at[n], cx_r.at[n], (r_other, c))

    def col_chunk(d, _):
        n = lax.rem(m + d, 8)
        out = lax.dot_general(
            resid[:, rows(n, C)], rowv[...], (((0,), (0,)), ((), ())), preferred_element_type=F32
        )

        @pl.when(core == 0)
        def _():
            cown[n] = out[:S]
            cxs[n] = out[S:].astype(BF16)

        @pl.when(core == 1)
        def _():
            cown[n] = out[S:]
            cxs[n] = out[:S].astype(BF16)

        cx_copy(n).start()
        return 0

    def cg_copy(n, slot):
        return remote(csend.at[n], crecv.at[slot], cg_s.at[n], cg_r.at[slot], (2 * n + core, c))

    def col_sum(d, _):
        n = lax.rem(m + d, 8)
        cx_copy(n).wait_recv()
        csend[n] = (cown[n] + cxr[n].astype(F32)).astype(BF16)
        cg_copy(n, m).start()
        return 0

    LAG = 3

    def forward_loop(p, _):
        chunk(p)

        @pl.when(p >= LAG)
        def _():
            reduce(p - LAG)

        return 0

    lax.fori_loop(0, NC, forward_loop, 0)
    lax.fori_loop(1, 5, col_chunk, 0)

    def reduce_loop(p, _):
        reduce(p)
        return 0

    lax.fori_loop(NC - LAG, NC, reduce_loop, 0)
    lax.fori_loop(1, 4, col_sum, 0)
    lax.fori_loop(5, 9, col_chunk, 0)
    lax.fori_loop(4, 8, col_sum, 0)
    cx_copy(m).wait_recv()
    grad = cown[m] + cxr[m].astype(F32)

    def col_recv(d, acc):
        n = lax.rem(m + d, 8)
        cg_copy(n, n).wait_recv()
        return acc + crecv[n].astype(F32)

    grad = lax.fori_loop(1, 8, col_recv, grad)

    def row_recv(d, acc):
        i = lax.rem(z + d, 8)

        @pl.when(i != z)
        def _():
            rg_copy(i, i).wait_recv()

        return acc + rrecv[i].astype(F32)

    grad = lax.fori_loop(0, 8, row_recv, grad)
    accn = acc_ref[...] + grad * grad
    accn_ref[...] = accn
    upd_ref[...] = (vec_ref[...].astype(F32) - 0.5 * grad / jnp.sqrt(accn)).astype(BF16)

    def sent(i, _):
        @pl.when(jnp.logical_not(jnp.logical_and(on_diag, i == z)))
        def _():
            rv_copy(i).wait_send()

        @pl.when(i != z)
        def _():
            rg_copy(i, z).wait_send()

        rf_copy(i).wait_send()
        cx_copy(i).wait_send()
        for half in range(2):

            @pl.when(jnp.logical_not(jnp.logical_and(stays, 2 * i + half == r)))
            def _():
                md_copy(2 * i + half).wait_send()

        @pl.when(i != m)
        def _():
            cg_copy(i, m).wait_send()

        @pl.when(i != 0)
        def _():
            cv_copy(i).wait_send()
            cf_copy(i).wait_send()

        return 0

    lax.fori_loop(0, 8, sent, 0)


def shards(counts, vectors, accum):
    vmem = pl.BlockSpec(memory_space=pltpu.VMEM)
    dma = pltpu.SemaphoreType.DMA
    many = dma((N,))
    eight = dma((8,))
    three = dma((3,))
    tile = pltpu.VMEM((8, 128), F32)
    tiles = pltpu.VMEM((8, 8, 128), F32)
    half = pltpu.VMEM((8, S, D), BF16)
    return pl.pallas_call(
        kernel,
        out_shape=(
            jax.ShapeDtypeStruct((S, D), BF16),
            jax.ShapeDtypeStruct((S, D), F32),
        ),
        in_specs=[pl.BlockSpec(memory_space=pl.ANY), vmem, vmem],
        out_specs=(vmem, vmem),
        scratch_shapes=[
            pltpu.VMEM((B, B), jnp.int32),
            pltpu.VMEM((B, D), BF16),
            pltpu.VMEM((B, D), BF16),
            pltpu.VMEM((B, B), F32),
            pltpu.VMEM((B, B), F32),
            pltpu.VMEM((B, B), BF16),
            pltpu.VMEM((C, B), F32),
            pltpu.VMEM((C, 128), F32),
            pltpu.VMEM((8, B), F32),
            pltpu.VMEM((B, 128), F32),
            tile, tile, tile, tile, tile, tile, tile, tile, tile, tiles, tiles, tiles,
            pltpu.VMEM((B, D), BF16), pltpu.VMEM((N, S, D), BF16), half, half,
            pltpu.VMEM((8, S, D), F32), half, half, half, half,
            eight, eight, many, eight, eight, many, eight,
            three, three, eight, eight, eight, eight, eight, eight,
            many, many, eight, eight, eight, eight, eight, eight,
        ],
        compiler_params=pltpu.CompilerParams(
            collective_id=1, has_side_effects=True, vmem_limit_bytes=48 * 2**20
        ),
        name="swivel_step",
    )(counts, vectors, accum)


def solution(mesh):
    return jax.shard_map(
        shards,
        mesh=mesh,
        in_specs=(P("row", "col"), P(("col", "row"), None), P(("col", "row"), None)),
        out_specs=(P(("col", "row"), None), P(("col", "row"), None)),
        check_vma=False,
    )
```

```python
import jax
import jax.numpy as jnp
from jax import lax
from jax.experimental import pallas as pl
from jax.experimental.pallas import tpu as pltpu
from jax.sharding import PartitionSpec as P

MESH = pl.DeviceIdType.MESH
F32 = jnp.float32
BF16 = jnp.bfloat16
N = 16
B = 1024
S = 64
D = 512
C = 128
NC = B // C


def rows(i, size):
    return pl.ds(pl.multiple_of(i * size, size), size)


def kernel(
    counts_ref, vec_ref, acc_ref, upd_ref, accn_ref,
    cnt, colv, zrow, rowv, logx, weight, resid, score, part, ct, rt,
    rs_mine, cs_mine, tot_mine, rs_two, cs_two, tot_two, rs_got, cs_got, tot_got, rs_all, cs_all, tot_all,
    rsend, mid, zsend, rrecv, cown, cxs, cxr, csend, crecv,
    cnt_sem, cv_s, cv_r, cf_s, zr_s, zr_r, rv_s, rv_r,
    pair_s, pair_r, rm_s, rm_r, cm_s, cm_r, tm_s, tm_r,
    md_s, md_r, rg_s, rg_r, cx_s, cx_r, cg_s, cg_r,
):
    r = lax.axis_index("row")
    c = lax.axis_index("col")
    m, core = r // 2, r % 2
    xh, y = m // 4, m % 4
    z, xl = c // 2, c % 2
    r_other = 2 * m + (1 - core)
    c_other = 2 * z + (1 - xl)
    stays = core == xl

    def remote(src, dst, ssem, rsem, dev):
        return pltpu.make_async_remote_copy(
            src_ref=src, dst_ref=dst, send_sem=ssem, recv_sem=rsem, device_id=dev, device_id_type=MESH
        )

    def near(p):
        return lax.rem(z + m + 8 - p, 8)

    def cnt_copy(k):
        return pltpu.make_async_copy(
            counts_ref.at[rows(k, C)], cnt.at[rows(k, C)], cnt_sem.at[k]
        )

    for k in range(NC):
        cnt_copy(k).start()

    barrier = pltpu.get_barrier_semaphore()

    def hello(dev):
        pl.semaphore_signal(barrier, inc=1, device_id=dev, device_id_type=MESH)

    def greet_plane(d, _):
        o = lax.rem(r + d, N)
        hello((o, c))
        hello((o, c_other))
        return 0

    hello((r, c_other))
    lax.fori_loop(1, N, greet_plane, 0)

    def greet(d, _):
        hello((r, 2 * lax.rem(z + d, 8) + xl))
        return 0

    lax.fori_loop(1, 8, greet, 0)

    col8 = jnp.zeros((8, B), F32)
    for k in range(NC):
        cnt_copy(k).wait()

        def strip(i, acc, k=k):
            x = cnt[rows(k * (C // 8) + i, 8), :].astype(F32)
            p = x[:, 0:128]
            for q in range(1, 8):
                p = p + x[:, q * 128 : (q + 1) * 128]
            part[rows(i, 8), :] = p
            return acc + x

        col8 = lax.fori_loop(0, C // 8, strip, col8, unroll=4)
        rs_mine[k : k + 1, :] = jnp.sum(part[...].T, axis=0, keepdims=True)
    col1 = jnp.sum(col8, axis=0, keepdims=True)
    for k in range(8):
        cs_mine[k : k + 1, :] = col1[:, k * 128 : (k + 1) * 128]

    pl.semaphore_wait(barrier, 38)

    pair_row = remote(rs_mine, rs_got, pair_s.at[0], pair_r.at[0], (r, c_other))
    pair_col = remote(cs_mine, cs_got, pair_s.at[1], pair_r.at[1], (r_other, c))
    pair_tot = remote(tot_mine, tot_got, pair_s.at[2], pair_r.at[2], (r_other, c))

    pair_row.start()
    pair_col.start()

    def zr_copy(i, slot):
        return remote(vec_ref, zrow.at[slot], zr_s.at[i], zr_r.at[slot], (r, 2 * i + xl))

    def zr_start(d, _):
        i = lax.rem(d + m - z + 8, 8)

        @pl.when(i != z)
        def _():
            zr_copy(i, z).start()

        return 0

    def rv_copy(i, half):
        return remote(
            zrow.at[i], rowv.at[rows(r, S)], rv_s.at[2 * i + half], rv_r.at[r], (2 * i + xl, 2 * z + half)
        )

    def rv_keeps(i, half):
        return jnp.logical_and(2 * i + xl == r, half == xl)

    def rv_send(i):
        for half in range(2):

            @pl.when(jnp.logical_not(rv_keeps(i, half)))
            def _():
                rv_copy(i, half).start()

            @pl.when(rv_keeps(i, half))
            def _():
                rowv[rows(r, S), :] = zrow[i]

    def rv_forward(p):
        i = lax.rem(p + m - z + 8, 8)

        @pl.when(i != z)
        def _():
            zr_copy(i, i).wait_recv()
            rv_send(i)

    lax.fori_loop(0, 8, zr_start, 0)
    zrow[z] = vec_ref[...]
    rv_send(z)

    def cv_copy(d):
        return remote(
            vec_ref, colv.at[rows(r, S)], cv_s.at[d], cv_r.at[r], (2 * lax.rem(m + d, 8) + core, c)
        )

    cv_core = remote(vec_ref, colv.at[rows(r, S)], cv_s.at[0], cv_r.at[r], (r_other, c))
    for d in range(1, 8):
        cv_copy(d).start()
    cv_core.start()
    colv[rows(r, S), :] = vec_ref[...]

    def cf_copy(d):
        o = 2 * lax.rem(m + d, 8) + core
        block = colv.at[rows(o, S)]
        return remote(block, block, cf_s.at[d], cv_r.at[o], (r_other, c))

    def cv_forward(d):
        cf_copy(d).wait_recv()
        cf_copy(d).start()

    def tile_copy(axis, src, dst, ssem, rsem, o, slot):
        dev = (2 * o + core, c) if axis == 0 else (r, 2 * o + xl)
        return remote(src, dst.at[slot], ssem.at[o], rsem.at[slot], dev)

    def spread(axis, src, dst, ssem, rsem):
        me = m if axis == 0 else z

        def one(d, _):
            tile_copy(axis, src, dst, ssem, rsem, lax.rem(me + d, 8), me).start()
            return 0

        lax.fori_loop(1, 8, one, 0)
        dst[me] = src[...]

    def collect(axis, src, dst, ssem, rsem):
        me = m if axis == 0 else z

        def one(d, _):
            o = lax.rem(me + d, 8)
            tile_copy(axis, src, dst, ssem, rsem, o, o).wait()
            return 0

        lax.fori_loop(1, 8, one, 0)
        return jnp.sum(dst[...], axis=0)

    rm = (1, rs_two, rs_all, rm_s, rm_r)
    cm = (0, cs_two, cs_all, cm_s, cm_r)
    tm = (0, tot_two, tot_all, tm_s, tm_r)

    def prep(i, _):
        x = cnt[rows(i, 8), :].astype(F32)
        logx[rows(i, 8), :] = jnp.log(jnp.maximum(x, 1.0))
        w = (1.0 / 32.0) * (0.1 + 0.25 * jnp.sqrt(x))
        weight[rows(i, 8), :] = jnp.where(x > 0.0, w, 0.0)
        return 0

    def prep_part(k):
        lax.fori_loop(k * 32, (k + 1) * 32, prep, 0, unroll=2)

    for k in range(4):
        prep_part(k)
    pair_row.wait()
    rs_two[...] = rs_mine[...] + rs_got[...]
    spread(*rm)
    pair_col.wait()
    cs_two[...] = cs_mine[...] + cs_got[...]
    spread(*cm)
    rv_forward(0)
    cv_forward(1)
    rv_forward(1)
    cv_forward(2)
    cv_forward(3)
    rv_forward(2)
    cv_forward(4)
    cv_forward(5)
    rsum = collect(*rm)
    tot_mine[...] = jnp.full((8, 128), jnp.sum(rsum), F32)
    pair_tot.start()
    rv_forward(3)
    cv_forward(6)
    cv_forward(7)
    pair_tot.wait()
    tot_two[...] = tot_mine[...] + tot_got[...]
    spread(*tm)
    rv_forward(4)
    rlog = jnp.log(rsum)
    for k in range(NC):
        rt[k * C : (k + 1) * C, :] = jnp.broadcast_to(rlog[k : k + 1, :], (C, 128)).T
    clog = jnp.log(collect(*cm))
    cv_core.wait_send()

    def cv_rest(d, _):
        o = 2 * lax.rem(m + d, 8) + 1 - core
        block = colv.at[rows(o, S)]
        remote(block, block, cf_s.at[0], cv_r.at[o], (r_other, c)).wait_recv()
        return 0

    lax.fori_loop(0, 8, cv_rest, 0)
    clog = clog - jnp.log(collect(*tm))
    for k in range(8):
        ct[0:1, k * 128 : (k + 1) * 128] = clog[k : k + 1, :]

    def md_copy(j):
        return remote(rsend.at[rows(j, S)], mid.at[2 * m + xl], md_s.at[j], md_r.at[2 * m + xl], (j, 2 * z + core))

    def chunk(p):
        n = near(p)
        here = rows(n, C)
        for half in range(2):
            j = 2 * n + half
            block = rowv.at[rows(j, S)]

            @pl.when(jnp.logical_not(jnp.logical_and(stays, j == r)))
            def _():
                remote(block, block, rv_s.at[j], rv_r.at[j], (r_other, c)).wait_recv()

        score[...] = lax.dot_general(
            rowv[here, :], colv[...], (((1,), (1,)), ((), ())), preferred_element_type=F32
        )

        def strip(i, _):
            at = rows(n * (C // 16) + i, 16)
            rl = rt[at, :]
            rl = jnp.concatenate([rl] * 8, axis=1)
            gap = score[rows(i, 16), :] - logx[at, :] + (rl + ct[0:1, :])
            w = weight[at, :]
            sig = (1.0 / 64.0) + (1.0 / 64.0) * jnp.tanh(0.5 * gap)
            resid[at, :] = jnp.where(w > 0.0, w * gap, sig).astype(BF16)
            return 0

        lax.fori_loop(0, C // 16, strip, 0, unroll=2)
        out = jnp.dot(resid[here, :], colv[...], preferred_element_type=F32)

        rsend[here, :] = out.astype(BF16)
        for half in range(2):
            mine = jnp.logical_and(stays, 2 * n + half == r)

            @pl.when(jnp.logical_not(mine))
            def _():
                md_copy(2 * n + half).start()

            @pl.when(mine)
            def _():
                mid[2 * m + xl] = rsend[rows(2 * n + half, S), :]

    def rg_copy(n, slot):
        return remote(zsend.at[n], rrecv.at[slot], rg_s.at[n], rg_r.at[slot], (r, 2 * n + xl))

    def reduce(p):
        n = lax.rem(m - z + p + 8, 8)
        for half in range(2):
            slot = 2 * n + half

            @pl.when(jnp.logical_not(jnp.logical_and(stays, slot == 2 * m + xl)))
            def _():
                remote(mid.at[slot], mid.at[slot], md_s.at[0], md_r.at[slot], (r_other, c)).wait_recv()

        zsend[n] = (mid[2 * n].astype(F32) + mid[2 * n + 1].astype(F32)).astype(BF16)

        @pl.when(n != z)
        def _():
            rg_copy(n, z).start()

        @pl.when(n == z)
        def _():
            rrecv[z] = zsend[n]

    def cx_copy(n):
        return remote(cxs.at[n], cxr.at[n], cx_s.at[n], cx_r.at[n], (r_other, c))

    def col_chunk(d, _):
        n = lax.rem(m + d, 8)
        out = lax.dot_general(
            resid[:, rows(n, C)], rowv[...], (((0,), (0,)), ((), ())), preferred_element_type=F32
        )

        @pl.when(core == 0)
        def _():
            cown[n] = out[:S]
            cxs[n] = out[S:].astype(BF16)

        @pl.when(core == 1)
        def _():
            cown[n] = out[S:]
            cxs[n] = out[:S].astype(BF16)

        cx_copy(n).start()
        return 0

    def cg_copy(n, slot):
        return remote(csend.at[n], crecv.at[slot], cg_s.at[n], cg_r.at[slot], (2 * n + core, c))

    def col_sum(d, _):
        n = lax.rem(m + d, 8)
        cx_copy(n).wait_recv()
        csend[n] = (cown[n] + cxr[n].astype(F32)).astype(BF16)
        cg_copy(n, m).start()
        return 0

    LAG = 6

    def forward_loop(p, _):
        @pl.when(p < 3)
        def _():
            rv_forward(p + 5)

        chunk(p)

        @pl.when(p >= LAG)
        def _():
            reduce(p - LAG)

        return 0

    lax.fori_loop(0, NC, forward_loop, 0)
    def reduce_loop(p, _):
        reduce(p)
        return 0

    lax.fori_loop(1, 5, col_chunk, 0)
    lax.fori_loop(NC - LAG, NC - 3, reduce_loop, 0)
    lax.fori_loop(5, 9, col_chunk, 0)
    lax.fori_loop(1, 8, col_sum, 0)
    lax.fori_loop(NC - 3, NC, reduce_loop, 0)
    cx_copy(m).wait_recv()
    grad = cown[m] + cxr[m].astype(F32)

    def col_recv(d, acc):
        n = lax.rem(m + d, 8)
        cg_copy(n, n).wait_recv()
        return acc + crecv[n].astype(F32)

    grad = lax.fori_loop(1, 8, col_recv, grad)

    def row_recv(d, acc):
        i = lax.rem(z + d, 8)

        @pl.when(i != z)
        def _():
            rg_copy(i, i).wait_recv()

        return acc + rrecv[i].astype(F32)

    grad = lax.fori_loop(0, 8, row_recv, grad)
    accn = acc_ref[...] + grad * grad
    accn_ref[...] = accn
    upd_ref[...] = (vec_ref[...].astype(F32) - 0.5 * grad / jnp.sqrt(accn)).astype(BF16)

    def sent(i, _):
        @pl.when(i != z)
        def _():
            zr_copy(i, z).wait_send()
            rg_copy(i, z).wait_send()

        cx_copy(i).wait_send()
        for half in range(2):

            @pl.when(jnp.logical_not(rv_keeps(i, half)))
            def _():
                rv_copy(i, half).wait_send()

            @pl.when(jnp.logical_not(jnp.logical_and(stays, 2 * i + half == r)))
            def _():
                md_copy(2 * i + half).wait_send()

        @pl.when(i != m)
        def _():
            cg_copy(i, m).wait_send()

        @pl.when(i != 0)
        def _():
            cv_copy(i).wait_send()
            cf_copy(i).wait_send()

        return 0

    lax.fori_loop(0, 8, sent, 0)


def shards(counts, vectors, accum):
    vmem = pl.BlockSpec(memory_space=pltpu.VMEM)
    dma = pltpu.SemaphoreType.DMA
    many = dma((N,))
    eight = dma((8,))
    three = dma((3,))
    tile = pltpu.VMEM((8, 128), F32)
    tiles = pltpu.VMEM((8, 8, 128), F32)
    half = pltpu.VMEM((8, S, D), BF16)
    return pl.pallas_call(
        kernel,
        out_shape=(
            jax.ShapeDtypeStruct((S, D), BF16),
            jax.ShapeDtypeStruct((S, D), F32),
        ),
        in_specs=[pl.BlockSpec(memory_space=pl.ANY), vmem, vmem],
        out_specs=(vmem, vmem),
        scratch_shapes=[
            pltpu.VMEM((B, B), jnp.int32),
            pltpu.VMEM((B, D), BF16),
            half,
            pltpu.VMEM((B, D), BF16),
            pltpu.VMEM((B, B), F32),
            pltpu.VMEM((B, B), F32),
            pltpu.VMEM((B, B), BF16),
            pltpu.VMEM((C, B), F32),
            pltpu.VMEM((C, 128), F32),
            pltpu.VMEM((8, B), F32),
            pltpu.VMEM((B, 128), F32),
            tile, tile, tile, tile, tile, tile, tile, tile, tile, tiles, tiles, tiles,
            pltpu.VMEM((B, D), BF16), pltpu.VMEM((N, S, D), BF16), half, half,
            pltpu.VMEM((8, S, D), F32), half, half, half, half,
            eight, eight, many, eight, eight, eight, many, many,
            three, three, eight, eight, eight, eight, eight, eight,
            many, many, eight, eight, eight, eight, eight, eight,
        ],
        compiler_params=pltpu.CompilerParams(
            collective_id=1, has_side_effects=True, vmem_limit_bytes=48 * 2**20
        ),
        name="swivel_step",
    )(counts, vectors, accum)


def solution(mesh):
    return jax.shard_map(
        shards,
        mesh=mesh,
        in_specs=(P("row", "col"), P(("col", "row"), None), P(("col", "row"), None)),
        out_specs=(P(("col", "row"), None), P(("col", "row"), None)),
        check_vma=False,
    )
```

```python
import jax
import jax.numpy as jnp
from jax import lax
from jax.experimental import pallas as pl
from jax.experimental.pallas import tpu as pltpu
from jax.sharding import PartitionSpec as P

MESH = pl.DeviceIdType.MESH
F32 = jnp.float32
BF16 = jnp.bfloat16
N = 16
B = 1024
S = 64
D = 512
C = 128
NC = B // C


def rows(i, size):
    return pl.ds(pl.multiple_of(i * size, size), size)


def kernel(
    counts_hbm, vec_hbm, grad_ref,
    vec_ref, cnt, colv, zrow, rowv, logx, weight, resid, score, part, ct, rt,
    rs_mine, cs_mine, tot_mine, rs_two, cs_two, tot_two, rs_got, cs_got, tot_got, rs_all, cs_all, tot_all,
    rsend, mid, zsend, rrecv, cown, cxs, cxr, csend, crecv,
    in_sem, cnt_sem, cv_s, cv_r, cf_s, zr_s, zr_r, rv_s, rv_r,
    pair_s, pair_r, rm_s, rm_r, cm_s, cm_r, tm_s, tm_r,
    md_s, md_r, rg_s, rg_r, cx_s, cx_r, cg_s, cg_r,
):
    r = lax.axis_index("row")
    c = lax.axis_index("col")
    m, core = r // 2, r % 2
    xh, y = m // 4, m % 4
    z, xl = c // 2, c % 2
    r_other = 2 * m + (1 - core)
    c_other = 2 * z + (1 - xl)
    stays = core == xl

    def remote(src, dst, ssem, rsem, dev):
        return pltpu.make_async_remote_copy(
            src_ref=src, dst_ref=dst, send_sem=ssem, recv_sem=rsem, device_id=dev, device_id_type=MESH
        )

    def near(p):
        return lax.rem(z + m + 8 - p, 8)

    def cnt_copy(k):
        return pltpu.make_async_copy(
            counts_hbm.at[rows(k, C)], cnt.at[rows(k, C)], cnt_sem.at[k]
        )

    vec_in = pltpu.make_async_copy(vec_hbm, vec_ref, in_sem)
    vec_in.start()
    for k in range(NC):
        cnt_copy(k).start()

    barrier = pltpu.get_barrier_semaphore()

    def hello(dev):
        pl.semaphore_signal(barrier, inc=1, device_id=dev, device_id_type=MESH)

    def greet_plane(d, _):
        o = lax.rem(r + d, N)
        hello((o, c))
        hello((o, c_other))
        return 0

    hello((r, c_other))
    lax.fori_loop(1, N, greet_plane, 0)

    def greet(d, _):
        hello((r, 2 * lax.rem(z + d, 8) + xl))
        return 0

    lax.fori_loop(1, 8, greet, 0)

    col8 = jnp.zeros((8, B), F32)
    for k in range(NC):
        cnt_copy(k).wait()

        def strip(i, acc, k=k):
            x = cnt[rows(k * (C // 8) + i, 8), :].astype(F32)
            p = x[:, 0:128]
            for q in range(1, 8):
                p = p + x[:, q * 128 : (q + 1) * 128]
            part[rows(i, 8), :] = p
            return acc + x

        col8 = lax.fori_loop(0, C // 8, strip, col8, unroll=4)
        rs_mine[k : k + 1, :] = jnp.sum(part[...].T, axis=0, keepdims=True)
    col1 = jnp.sum(col8, axis=0, keepdims=True)
    for k in range(8):
        cs_mine[k : k + 1, :] = col1[:, k * 128 : (k + 1) * 128]

    vec_in.wait()
    pl.semaphore_wait(barrier, 38)

    pair_row = remote(rs_mine, rs_got, pair_s.at[0], pair_r.at[0], (r, c_other))
    pair_col = remote(cs_mine, cs_got, pair_s.at[1], pair_r.at[1], (r_other, c))
    pair_tot = remote(tot_mine, tot_got, pair_s.at[2], pair_r.at[2], (r_other, c))

    pair_row.start()
    pair_col.start()

    def zr_copy(i, slot):
        return remote(vec_ref, zrow.at[slot], zr_s.at[i], zr_r.at[slot], (r, 2 * i + xl))

    def zr_start(d, _):
        i = lax.rem(d + m - z + 8, 8)

        @pl.when(i != z)
        def _():
            zr_copy(i, z).start()

        return 0

    def rv_copy(i, half):
        return remote(
            zrow.at[i], rowv.at[rows(r, S)], rv_s.at[2 * i + half], rv_r.at[r], (2 * i + xl, 2 * z + half)
        )

    def rv_keeps(i, half):
        return jnp.logical_and(2 * i + xl == r, half == xl)

    def rv_send(i):
        for half in range(2):

            @pl.when(jnp.logical_not(rv_keeps(i, half)))
            def _():
                rv_copy(i, half).start()

            @pl.when(rv_keeps(i, half))
            def _():
                rowv[rows(r, S), :] = zrow[i]

    def rv_forward(p):
        i = lax.rem(p + m - z + 8, 8)

        @pl.when(i != z)
        def _():
            zr_copy(i, i).wait_recv()
            rv_send(i)

    lax.fori_loop(0, 8, zr_start, 0)
    zrow[z] = vec_ref[...]
    rv_send(z)

    def cv_copy(d):
        return remote(
            vec_ref, colv.at[rows(r, S)], cv_s.at[d], cv_r.at[r], (2 * lax.rem(m + d, 8) + core, c)
        )

    cv_core = remote(vec_ref, colv.at[rows(r, S)], cv_s.at[0], cv_r.at[r], (r_other, c))
    for d in range(1, 8):
        cv_copy(d).start()
    cv_core.start()
    colv[rows(r, S), :] = vec_ref[...]

    def cf_copy(d):
        o = 2 * lax.rem(m + d, 8) + core
        block = colv.at[rows(o, S)]
        return remote(block, block, cf_s.at[d], cv_r.at[o], (r_other, c))

    def cv_forward(d):
        cf_copy(d).wait_recv()
        cf_copy(d).start()

    def tile_copy(axis, src, dst, ssem, rsem, o, slot):
        dev = (2 * o + core, c) if axis == 0 else (r, 2 * o + xl)
        return remote(src, dst.at[slot], ssem.at[o], rsem.at[slot], dev)

    def spread(axis, src, dst, ssem, rsem):
        me = m if axis == 0 else z

        def one(d, _):
            tile_copy(axis, src, dst, ssem, rsem, lax.rem(me + d, 8), me).start()
            return 0

        lax.fori_loop(1, 8, one, 0)
        dst[me] = src[...]

    def collect(axis, src, dst, ssem, rsem):
        me = m if axis == 0 else z

        def one(d, _):
            o = lax.rem(me + d, 8)
            tile_copy(axis, src, dst, ssem, rsem, o, o).wait()
            return 0

        lax.fori_loop(1, 8, one, 0)
        return jnp.sum(dst[...], axis=0)

    rm = (1, rs_two, rs_all, rm_s, rm_r)
    cm = (0, cs_two, cs_all, cm_s, cm_r)
    tm = (0, tot_two, tot_all, tm_s, tm_r)

    def prep(i, _):
        x = cnt[rows(i, 8), :].astype(F32)
        logx[rows(i, 8), :] = jnp.log(jnp.maximum(x, 1.0))
        w = (1.0 / 32.0) * (0.1 + 0.25 * jnp.sqrt(x))
        weight[rows(i, 8), :] = jnp.where(x > 0.0, w, 0.0)
        return 0

    def prep_part(k):
        lax.fori_loop(k * 32, (k + 1) * 32, prep, 0, unroll=2)

    for k in range(4):
        prep_part(k)
    pair_row.wait()
    rs_two[...] = rs_mine[...] + rs_got[...]
    spread(*rm)
    pair_col.wait()
    cs_two[...] = cs_mine[...] + cs_got[...]
    spread(*cm)
    rv_forward(0)
    cv_forward(1)
    rv_forward(1)
    cv_forward(2)
    cv_forward(3)
    rv_forward(2)
    cv_forward(4)
    cv_forward(5)
    rsum = collect(*rm)
    tot_mine[...] = jnp.full((8, 128), jnp.sum(rsum), F32)
    pair_tot.start()
    rv_forward(3)
    cv_forward(6)
    cv_forward(7)
    pair_tot.wait()
    tot_two[...] = tot_mine[...] + tot_got[...]
    spread(*tm)
    rv_forward(4)
    rlog = jnp.log(rsum)
    for k in range(NC):
        rt[k * C : (k + 1) * C, :] = jnp.broadcast_to(rlog[k : k + 1, :], (C, 128)).T
    clog = jnp.log(collect(*cm))
    cv_core.wait_send()

    def cv_rest(d, _):
        o = 2 * lax.rem(m + d, 8) + 1 - core
        block = colv.at[rows(o, S)]
        remote(block, block, cf_s.at[0], cv_r.at[o], (r_other, c)).wait_recv()
        return 0

    lax.fori_loop(0, 8, cv_rest, 0)
    clog = clog - jnp.log(collect(*tm))
    for k in range(8):
        ct[0:1, k * 128 : (k + 1) * 128] = clog[k : k + 1, :]

    def md_copy(j):
        return remote(rsend.at[rows(j, S)], mid.at[2 * m + xl], md_s.at[j], md_r.at[2 * m + xl], (j, 2 * z + core))

    def chunk(p):
        n = near(p)
        here = rows(n, C)
        for half in range(2):
            j = 2 * n + half
            block = rowv.at[rows(j, S)]

            @pl.when(jnp.logical_not(jnp.logical_and(stays, j == r)))
            def _():
                remote(block, block, rv_s.at[j], rv_r.at[j], (r_other, c)).wait_recv()

        score[...] = lax.dot_general(
            rowv[here, :], colv[...], (((1,), (1,)), ((), ())), preferred_element_type=F32
        )

        def strip(i, _):
            at = rows(n * (C // 16) + i, 16)
            rl = rt[at, :]
            rl = jnp.concatenate([rl] * 8, axis=1)
            gap = score[rows(i, 16), :] - logx[at, :] + (rl + ct[0:1, :])
            w = weight[at, :]
            sig = (1.0 / 64.0) + (1.0 / 64.0) * jnp.tanh(0.5 * gap)
            resid[at, :] = jnp.where(w > 0.0, w * gap, sig).astype(BF16)
            return 0

        lax.fori_loop(0, C // 16, strip, 0, unroll=4)
        out = jnp.dot(resid[here, :], colv[...], preferred_element_type=F32)

        rsend[here, :] = out.astype(BF16)
        for half in range(2):
            mine = jnp.logical_and(stays, 2 * n + half == r)

            @pl.when(jnp.logical_not(mine))
            def _():
                md_copy(2 * n + half).start()

            @pl.when(mine)
            def _():
                mid[2 * m + xl] = rsend[rows(2 * n + half, S), :]

    def rg_copy(n, slot):
        return remote(zsend.at[n], rrecv.at[slot], rg_s.at[n], rg_r.at[slot], (r, 2 * n + xl))

    def reduce(p):
        n = lax.rem(m - z + p + 8, 8)
        for half in range(2):
            slot = 2 * n + half

            @pl.when(jnp.logical_not(jnp.logical_and(stays, slot == 2 * m + xl)))
            def _():
                remote(mid.at[slot], mid.at[slot], md_s.at[0], md_r.at[slot], (r_other, c)).wait_recv()

        zsend[n] = (mid[2 * n].astype(F32) + mid[2 * n + 1].astype(F32)).astype(BF16)

        @pl.when(n != z)
        def _():
            rg_copy(n, z).start()

        @pl.when(n == z)
        def _():
            rrecv[z] = zsend[n]

    def cx_copy(n):
        return remote(cxs.at[n], cxr.at[n], cx_s.at[n], cx_r.at[n], (r_other, c))

    def col_chunk(d, _):
        n = lax.rem(m + d, 8)
        out = lax.dot_general(
            resid[:, rows(n, C)], rowv[...], (((0,), (0,)), ((), ())), preferred_element_type=F32
        )

        @pl.when(core == 0)
        def _():
            cown[n] = out[:S]
            cxs[n] = out[S:].astype(BF16)

        @pl.when(core == 1)
        def _():
            cown[n] = out[S:]
            cxs[n] = out[:S].astype(BF16)

        cx_copy(n).start()
        return 0

    def cg_copy(n, slot):
        return remote(csend.at[n], crecv.at[slot], cg_s.at[n], cg_r.at[slot], (2 * n + core, c))

    def col_sum(d, _):
        n = lax.rem(m + d, 8)
        cx_copy(n).wait_recv()
        csend[n] = (cown[n] + cxr[n].astype(F32)).astype(BF16)
        cg_copy(n, m).start()
        return 0

    LAG = 6

    def forward_loop(p, _):
        @pl.when(p < 3)
        def _():
            rv_forward(p + 5)

        chunk(p)

        @pl.when(p >= LAG)
        def _():
            reduce(p - LAG)

        return 0

    lax.fori_loop(0, NC, forward_loop, 0)
    def reduce_loop(p, _):
        reduce(p)
        return 0

    lax.fori_loop(1, 5, col_chunk, 0)
    lax.fori_loop(NC - LAG, NC - 3, reduce_loop, 0)
    lax.fori_loop(5, 9, col_chunk, 0)
    lax.fori_loop(1, 8, col_sum, 0)
    lax.fori_loop(NC - 3, NC, reduce_loop, 0)
    cx_copy(m).wait_recv()
    grad = cown[m] + cxr[m].astype(F32)

    def col_recv(d, acc):
        n = lax.rem(m + d, 8)
        cg_copy(n, n).wait_recv()
        return acc + crecv[n].astype(F32)

    grad = lax.fori_loop(1, 8, col_recv, grad)

    def row_recv(d, acc):
        i = lax.rem(z + d, 8)

        @pl.when(i != z)
        def _():
            rg_copy(i, i).wait_recv()

        return acc + rrecv[i].astype(F32)

    grad = lax.fori_loop(0, 8, row_recv, grad)
    grad_ref[...] = grad

    def sent(i, _):
        @pl.when(i != z)
        def _():
            zr_copy(i, z).wait_send()
            rg_copy(i, z).wait_send()

        cx_copy(i).wait_send()
        for half in range(2):

            @pl.when(jnp.logical_not(rv_keeps(i, half)))
            def _():
                rv_copy(i, half).wait_send()

            @pl.when(jnp.logical_not(jnp.logical_and(stays, 2 * i + half == r)))
            def _():
                md_copy(2 * i + half).wait_send()

        @pl.when(i != m)
        def _():
            cg_copy(i, m).wait_send()

        @pl.when(i != 0)
        def _():
            cv_copy(i).wait_send()
            cf_copy(i).wait_send()

        return 0

    lax.fori_loop(0, 8, sent, 0)


def shards(counts, vectors, accum):
    vmem = pl.BlockSpec(memory_space=pltpu.VMEM)
    hbm = pl.BlockSpec(memory_space=pltpu.HBM)
    dma = pltpu.SemaphoreType.DMA
    many = dma((N,))
    eight = dma((8,))
    three = dma((3,))
    tile = pltpu.VMEM((8, 128), F32)
    tiles = pltpu.VMEM((8, 8, 128), F32)
    half = pltpu.VMEM((8, S, D), BF16)
    grad = pl.pallas_call(
        kernel,
        out_shape=jax.ShapeDtypeStruct((S, D), F32),
        in_specs=[hbm, hbm],
        out_specs=vmem,
        scratch_shapes=[
            pltpu.VMEM((S, D), BF16),
            pltpu.VMEM((B, B), jnp.int32),
            pltpu.VMEM((B, D), BF16),
            half,
            pltpu.VMEM((B, D), BF16),
            pltpu.VMEM((B, B), F32),
            pltpu.VMEM((B, B), F32),
            pltpu.VMEM((B, B), BF16),
            pltpu.VMEM((C, B), F32),
            pltpu.VMEM((C, 128), F32),
            pltpu.VMEM((8, B), F32),
            pltpu.VMEM((B, 128), F32),
            tile, tile, tile, tile, tile, tile, tile, tile, tile, tiles, tiles, tiles,
            pltpu.VMEM((B, D), BF16), pltpu.VMEM((N, S, D), BF16), half, half,
            pltpu.VMEM((8, S, D), F32), half, half, half, half,
            dma(()), eight, eight, many, eight, eight, eight, many, many,
            three, three, eight, eight, eight, eight, eight, eight,
            many, many, eight, eight, eight, eight, eight, eight,
        ],
        compiler_params=pltpu.CompilerParams(
            collective_id=1, has_side_effects=True, vmem_limit_bytes=50 * 2**20
        ),
        name="swivel_step",
    )(counts, vectors)
    accum_new = accum + grad * grad
    updated = (vectors.astype(F32) - 0.5 * grad / jnp.sqrt(accum_new)).astype(BF16)
    return updated, accum_new


def solution(mesh):
    return jax.shard_map(
        shards,
        mesh=mesh,
        in_specs=(P("row", "col"), P(("col", "row"), None), P(("col", "row"), None)),
        out_specs=(P(("col", "row"), None), P(("col", "row"), None)),
        check_vma=False,
    )
```

```python
import jax
import jax.numpy as jnp
from jax import lax
from jax.experimental import pallas as pl
from jax.experimental.pallas import tpu as pltpu
from jax.sharding import PartitionSpec as P

MESH = pl.DeviceIdType.MESH
F32 = jnp.float32
BF16 = jnp.bfloat16
N = 16
B = 1024
S = 64
D = 512
C = 128
NC = B // C


def rows(i, size):
    return pl.ds(pl.multiple_of(i * size, size), size)


def kernel(
    counts_hbm, vec_hbm, grad_ref,
    vec_ref, cnt, colv, zrow, rowv, logx, weight, resid, score, part, ct, rt,
    rs_mine, cs_mine, tot_mine, rs_two, cs_two, tot_two, rs_got, cs_got, tot_got, rs_all, cs_all, tot_all,
    rsend, mid, zsend, rrecv, cown, cxs, cxr, csend, crecv,
    in_sem, cnt_sem, cv_s, cv_r, cf_s, zr_s, zr_r, rv_s, rv_r,
    pair_s, pair_r, rm_s, rm_r, cm_s, cm_r, tm_s, tm_r,
    md_s, md_r, rg_s, rg_r, cx_s, cx_r, cg_s, cg_r,
):
    r = lax.axis_index("row")
    c = lax.axis_index("col")
    m, core = r // 2, r % 2
    xh, y = m // 4, m % 4
    z, xl = c // 2, c % 2
    r_other = 2 * m + (1 - core)
    c_other = 2 * z + (1 - xl)
    stays = core == xl

    def remote(src, dst, ssem, rsem, dev):
        return pltpu.make_async_remote_copy(
            src_ref=src, dst_ref=dst, send_sem=ssem, recv_sem=rsem, device_id=dev, device_id_type=MESH
        )

    def near(p):
        return lax.rem(z + m + 8 - p, 8)

    def cnt_copy(k):
        return pltpu.make_async_copy(
            counts_hbm.at[rows(k, C)], cnt.at[rows(k, C)], cnt_sem.at[k]
        )

    vec_in = pltpu.make_async_copy(vec_hbm, vec_ref, in_sem)
    vec_in.start()
    for k in range(NC):
        cnt_copy(k).start()

    barrier = pltpu.get_barrier_semaphore()

    def hello(dev):
        pl.semaphore_signal(barrier, inc=1, device_id=dev, device_id_type=MESH)

    def greet_plane(d, _):
        o = lax.rem(r + d, N)
        hello((o, c))
        hello((o, c_other))
        return 0

    hello((r, c_other))
    lax.fori_loop(1, N, greet_plane, 0)

    def greet(d, _):
        hello((r, 2 * lax.rem(z + d, 8) + xl))
        return 0

    lax.fori_loop(1, 8, greet, 0)

    col8 = jnp.zeros((8, B), F32)
    for k in range(NC):
        cnt_copy(k).wait()

        def strip(i, acc, k=k):
            x = cnt[rows(k * (C // 8) + i, 8), :].astype(F32)
            p = x[:, 0:128]
            for q in range(1, 8):
                p = p + x[:, q * 128 : (q + 1) * 128]
            part[rows(i, 8), :] = p
            return acc + x

        col8 = lax.fori_loop(0, C // 8, strip, col8, unroll=4)
        rs_mine[k : k + 1, :] = jnp.sum(part[...].T, axis=0, keepdims=True)
    col1 = jnp.sum(col8, axis=0, keepdims=True)
    for k in range(8):
        cs_mine[k : k + 1, :] = col1[:, k * 128 : (k + 1) * 128]

    vec_in.wait()
    pl.semaphore_wait(barrier, 38)

    pair_row = remote(rs_mine, rs_got, pair_s.at[0], pair_r.at[0], (r, c_other))
    pair_col = remote(cs_mine, cs_got, pair_s.at[1], pair_r.at[1], (r_other, c))
    pair_tot = remote(tot_mine, tot_got, pair_s.at[2], pair_r.at[2], (r_other, c))

    pair_row.start()
    pair_col.start()

    def zr_copy(i, slot):
        return remote(vec_ref, zrow.at[slot], zr_s.at[i], zr_r.at[slot], (r, 2 * i + xl))

    def zr_start(d, _):
        i = lax.rem(d + m - z + 8, 8)

        @pl.when(i != z)
        def _():
            zr_copy(i, z).start()

        return 0

    def rv_copy(i, half):
        return remote(
            zrow.at[i], rowv.at[rows(r, S)], rv_s.at[2 * i + half], rv_r.at[r], (2 * i + xl, 2 * z + half)
        )

    def rv_keeps(i, half):
        return jnp.logical_and(2 * i + xl == r, half == xl)

    def rv_send(i):
        for half in range(2):

            @pl.when(jnp.logical_not(rv_keeps(i, half)))
            def _():
                rv_copy(i, half).start()

            @pl.when(rv_keeps(i, half))
            def _():
                rowv[rows(r, S), :] = zrow[i]

    def rv_forward(p):
        i = lax.rem(p + m - z + 8, 8)

        @pl.when(i != z)
        def _():
            zr_copy(i, i).wait_recv()
            rv_send(i)

    lax.fori_loop(0, 8, zr_start, 0)
    zrow[z] = vec_ref[...]
    rv_send(z)

    def cv_copy(d):
        return remote(
            vec_ref, colv.at[rows(r, S)], cv_s.at[d], cv_r.at[r], (2 * lax.rem(m + d, 8) + core, c)
        )

    cv_core = remote(vec_ref, colv.at[rows(r, S)], cv_s.at[0], cv_r.at[r], (r_other, c))
    for d in range(1, 8):
        cv_copy(d).start()
    cv_core.start()
    colv[rows(r, S), :] = vec_ref[...]

    def cf_copy(d):
        o = 2 * lax.rem(m + d, 8) + core
        block = colv.at[rows(o, S)]
        return remote(block, block, cf_s.at[d], cv_r.at[o], (r_other, c))

    def cv_forward(d):
        cf_copy(d).wait_recv()
        cf_copy(d).start()

    def tile_copy(axis, src, dst, ssem, rsem, o, slot):
        dev = (2 * o + core, c) if axis == 0 else (r, 2 * o + xl)
        return remote(src, dst.at[slot], ssem.at[o], rsem.at[slot], dev)

    def spread(axis, src, dst, ssem, rsem):
        me = m if axis == 0 else z

        def one(d, _):
            tile_copy(axis, src, dst, ssem, rsem, lax.rem(me + d, 8), me).start()
            return 0

        lax.fori_loop(1, 8, one, 0)
        dst[me] = src[...]

    def collect(axis, src, dst, ssem, rsem):
        me = m if axis == 0 else z

        def one(d, _):
            o = lax.rem(me + d, 8)
            tile_copy(axis, src, dst, ssem, rsem, o, o).wait()
            return 0

        lax.fori_loop(1, 8, one, 0)
        return jnp.sum(dst[...], axis=0)

    rm = (1, rs_two, rs_all, rm_s, rm_r)
    cm = (0, cs_two, cs_all, cm_s, cm_r)
    tm = (0, tot_two, tot_all, tm_s, tm_r)

    def prep(i, _):
        x = cnt[rows(i, 8), :].astype(F32)
        logx[rows(i, 8), :] = jnp.log(jnp.maximum(x, 1.0))
        w = (1.0 / 32.0) * (0.1 + 0.25 * jnp.sqrt(x))
        weight[rows(i, 8), :] = jnp.where(x > 0.0, w, 0.0)
        return 0

    def prep_part(k):
        lax.fori_loop(k * 32, (k + 1) * 32, prep, 0, unroll=2)

    for k in range(4):
        prep_part(k)
    pair_row.wait()
    rs_two[...] = rs_mine[...] + rs_got[...]
    spread(*rm)
    pair_col.wait()
    cs_two[...] = cs_mine[...] + cs_got[...]
    spread(*cm)
    rv_forward(0)
    cv_forward(1)
    rv_forward(1)
    cv_forward(2)
    cv_forward(3)
    rv_forward(2)
    cv_forward(4)
    cv_forward(5)
    rsum = collect(*rm)
    tot_mine[...] = jnp.full((8, 128), jnp.sum(rsum), F32)
    pair_tot.start()
    rv_forward(3)
    cv_forward(6)
    cv_forward(7)
    pair_tot.wait()
    tot_two[...] = tot_mine[...] + tot_got[...]
    spread(*tm)
    rv_forward(4)
    rv_forward(5)
    rlog = jnp.log(rsum)
    for k in range(NC):
        rt[k * C : (k + 1) * C, :] = jnp.broadcast_to(rlog[k : k + 1, :], (C, 128)).T
    clog = jnp.log(collect(*cm))
    cv_core.wait_send()

    def cv_rest(d, _):
        o = 2 * lax.rem(m + d, 8) + 1 - core
        block = colv.at[rows(o, S)]
        remote(block, block, cf_s.at[0], cv_r.at[o], (r_other, c)).wait_recv()
        return 0

    lax.fori_loop(0, 8, cv_rest, 0)
    clog = clog - jnp.log(collect(*tm))
    for k in range(8):
        ct[0:1, k * 128 : (k + 1) * 128] = clog[k : k + 1, :]

    def md_copy(j):
        return remote(rsend.at[rows(j, S)], mid.at[2 * m + xl], md_s.at[j], md_r.at[2 * m + xl], (j, 2 * z + core))

    def chunk(p):
        n = near(p)
        here = rows(n, C)
        for half in range(2):
            j = 2 * n + half
            block = rowv.at[rows(j, S)]

            @pl.when(jnp.logical_not(jnp.logical_and(stays, j == r)))
            def _():
                remote(block, block, rv_s.at[j], rv_r.at[j], (r_other, c)).wait_recv()

        score[...] = lax.dot_general(
            rowv[here, :], colv[...], (((1,), (1,)), ((), ())), preferred_element_type=F32
        )

        def strip(i, _):
            at = rows(n * (C // 16) + i, 16)
            rl = rt[at, :]
            rl = jnp.concatenate([rl] * 8, axis=1)
            gap = score[rows(i, 16), :] - logx[at, :] + (rl + ct[0:1, :])
            w = weight[at, :]
            sig = (1.0 / 64.0) + (1.0 / 64.0) * jnp.tanh(0.5 * gap)
            resid[at, :] = jnp.where(w > 0.0, w * gap, sig).astype(BF16)
            return 0

        lax.fori_loop(0, C // 16, strip, 0, unroll=4)
        out = jnp.dot(resid[here, :], colv[...], preferred_element_type=F32)

        rsend[here, :] = out.astype(BF16)
        for half in range(2):
            mine = jnp.logical_and(stays, 2 * n + half == r)

            @pl.when(jnp.logical_not(mine))
            def _():
                md_copy(2 * n + half).start()

            @pl.when(mine)
            def _():
                mid[2 * m + xl] = rsend[rows(2 * n + half, S), :]

    def rg_copy(n, slot):
        return remote(zsend.at[n], rrecv.at[slot], rg_s.at[n], rg_r.at[slot], (r, 2 * n + xl))

    def reduce(p):
        n = lax.rem(m - z + p + 8, 8)
        for half in range(2):
            slot = 2 * n + half

            @pl.when(jnp.logical_not(jnp.logical_and(stays, slot == 2 * m + xl)))
            def _():
                remote(mid.at[slot], mid.at[slot], md_s.at[0], md_r.at[slot], (r_other, c)).wait_recv()

        zsend[n] = (mid[2 * n].astype(F32) + mid[2 * n + 1].astype(F32)).astype(BF16)

        @pl.when(n != z)
        def _():
            rg_copy(n, z).start()

        @pl.when(n == z)
        def _():
            rrecv[z] = zsend[n]

    def cx_copy(n):
        return remote(cxs.at[n], cxr.at[n], cx_s.at[n], cx_r.at[n], (r_other, c))

    def col_chunk(d, _):
        n = lax.rem(m + d, 8)
        out = lax.dot_general(
            resid[:, rows(n, C)], rowv[...], (((0,), (0,)), ((), ())), preferred_element_type=F32
        )

        @pl.when(core == 0)
        def _():
            cown[n] = out[:S]
            cxs[n] = out[S:].astype(BF16)

        @pl.when(core == 1)
        def _():
            cown[n] = out[S:]
            cxs[n] = out[:S].astype(BF16)

        cx_copy(n).start()
        return 0

    def cg_copy(n, slot):
        return remote(csend.at[n], crecv.at[slot], cg_s.at[n], cg_r.at[slot], (2 * n + core, c))

    def col_sum(d, _):
        n = lax.rem(m + d, 8)
        cx_copy(n).wait_recv()
        csend[n] = (cown[n] + cxr[n].astype(F32)).astype(BF16)
        cg_copy(n, m).start()
        return 0

    LAG = 6

    def forward_loop(p, _):
        @pl.when(p < 2)
        def _():
            rv_forward(p + 6)

        chunk(p)

        @pl.when(p >= LAG)
        def _():
            reduce(p - LAG)

        return 0

    lax.fori_loop(0, NC, forward_loop, 0)
    def reduce_loop(p, _):
        reduce(p)
        return 0

    lax.fori_loop(1, 5, col_chunk, 0)
    lax.fori_loop(NC - LAG, NC - 3, reduce_loop, 0)
    lax.fori_loop(5, 9, col_chunk, 0)
    lax.fori_loop(1, 8, col_sum, 0)
    lax.fori_loop(NC - 3, NC, reduce_loop, 0)
    cx_copy(m).wait_recv()
    grad = cown[m] + cxr[m].astype(F32)

    def col_recv(d, acc):
        n = lax.rem(m + d, 8)
        cg_copy(n, n).wait_recv()
        return acc + crecv[n].astype(F32)

    grad = lax.fori_loop(1, 8, col_recv, grad)

    def row_recv(d, acc):
        i = lax.rem(z + d, 8)

        @pl.when(i != z)
        def _():
            rg_copy(i, i).wait_recv()

        return acc + rrecv[i].astype(F32)

    grad = lax.fori_loop(0, 8, row_recv, grad)
    grad_ref[...] = grad

    def sent(i, _):
        @pl.when(i != z)
        def _():
            zr_copy(i, z).wait_send()
            rg_copy(i, z).wait_send()

        cx_copy(i).wait_send()
        for half in range(2):

            @pl.when(jnp.logical_not(rv_keeps(i, half)))
            def _():
                rv_copy(i, half).wait_send()

            @pl.when(jnp.logical_not(jnp.logical_and(stays, 2 * i + half == r)))
            def _():
                md_copy(2 * i + half).wait_send()

        @pl.when(i != m)
        def _():
            cg_copy(i, m).wait_send()

        @pl.when(i != 0)
        def _():
            cv_copy(i).wait_send()
            cf_copy(i).wait_send()

        return 0

    lax.fori_loop(0, 8, sent, 0)


def shards(counts, vectors, accum):
    vmem = pl.BlockSpec(memory_space=pltpu.VMEM)
    hbm = pl.BlockSpec(memory_space=pltpu.HBM)
    dma = pltpu.SemaphoreType.DMA
    many = dma((N,))
    eight = dma((8,))
    three = dma((3,))
    tile = pltpu.VMEM((8, 128), F32)
    tiles = pltpu.VMEM((8, 8, 128), F32)
    half = pltpu.VMEM((8, S, D), BF16)
    grad = pl.pallas_call(
        kernel,
        out_shape=jax.ShapeDtypeStruct((S, D), F32),
        in_specs=[hbm, hbm],
        out_specs=vmem,
        scratch_shapes=[
            pltpu.VMEM((S, D), BF16),
            pltpu.VMEM((B, B), jnp.int32),
            pltpu.VMEM((B, D), BF16),
            half,
            pltpu.VMEM((B, D), BF16),
            pltpu.VMEM((B, B), F32),
            pltpu.VMEM((B, B), F32),
            pltpu.VMEM((B, B), BF16),
            pltpu.VMEM((C, B), F32),
            pltpu.VMEM((C, 128), F32),
            pltpu.VMEM((8, B), F32),
            pltpu.VMEM((B, 128), F32),
            tile, tile, tile, tile, tile, tile, tile, tile, tile, tiles, tiles, tiles,
            pltpu.VMEM((B, D), BF16), pltpu.VMEM((N, S, D), BF16), half, half,
            pltpu.VMEM((8, S, D), F32), half, half, half, half,
            dma(()), eight, eight, many, eight, eight, eight, many, many,
            three, three, eight, eight, eight, eight, eight, eight,
            many, many, eight, eight, eight, eight, eight, eight,
        ],
        compiler_params=pltpu.CompilerParams(
            collective_id=1, has_side_effects=True, vmem_limit_bytes=50 * 2**20
        ),
        name="swivel_step",
    )(counts, vectors)
    accum_new = accum + grad * grad
    updated = (vectors.astype(F32) - 0.5 * grad / jnp.sqrt(accum_new)).astype(BF16)
    return updated, accum_new


def solution(mesh):
    return jax.shard_map(
        shards,
        mesh=mesh,
        in_specs=(P("row", "col"), P(("col", "row"), None), P(("col", "row"), None)),
        out_specs=(P(("col", "row"), None), P(("col", "row"), None)),
        check_vma=False,
    )
```

```python
import jax
import jax.numpy as jnp
from jax import lax
from jax.experimental import pallas as pl
from jax.experimental.pallas import tpu as pltpu
from jax.sharding import PartitionSpec as P

MESH = pl.DeviceIdType.MESH
F32 = jnp.float32
BF16 = jnp.bfloat16
N = 16
B = 1024
S = 64
D = 512
C = 128
NC = B // C


def rows(i, size):
    return pl.ds(pl.multiple_of(i * size, size), size)


def kernel(
    counts_hbm, vec_hbm, grad_ref,
    vec_ref, cnt, colv, zrow, rowv, logx, weight, resid, score, part, ct, rt,
    rs_mine, cs_mine, tot_mine, rs_two, cs_two, tot_two, rs_got, cs_got, tot_got, rs_all, cs_all, tot_all,
    rsend, mid, zsend, rrecv, cown, cxs, cxr, csend, crecv,
    in_sem, cnt_sem, cv_s, cv_r, cf_s, zr_s, zr_r, rv_s, rv_r,
    pair_s, pair_r, rm_s, rm_r, cm_s, cm_r, tm_s, tm_r,
    md_s, md_r, rg_s, rg_r, cx_s, cx_r, cg_s, cg_r,
):
    r = lax.axis_index("row")
    c = lax.axis_index("col")
    m, core = r // 2, r % 2
    xh, y = m // 4, m % 4
    z, xl = c // 2, c % 2
    r_other = 2 * m + (1 - core)
    c_other = 2 * z + (1 - xl)
    stays = core == xl

    def remote(src, dst, ssem, rsem, dev):
        return pltpu.make_async_remote_copy(
            src_ref=src, dst_ref=dst, send_sem=ssem, recv_sem=rsem, device_id=dev, device_id_type=MESH
        )

    def near(p):
        return lax.rem(z + m + 8 - p, 8)

    def cnt_copy(k):
        return pltpu.make_async_copy(
            counts_hbm.at[rows(k, C)], cnt.at[rows(k, C)], cnt_sem.at[k]
        )

    vec_in = pltpu.make_async_copy(vec_hbm, vec_ref, in_sem)
    vec_in.start()
    for k in range(NC):
        cnt_copy(k).start()

    barrier = pltpu.get_barrier_semaphore()

    def hello(dev):
        pl.semaphore_signal(barrier, inc=1, device_id=dev, device_id_type=MESH)

    def greet_plane(d, _):
        o = lax.rem(r + d, N)
        hello((o, c))
        hello((o, c_other))
        return 0

    hello((r, c_other))
    lax.fori_loop(1, N, greet_plane, 0)

    def greet(d, _):
        hello((r, 2 * lax.rem(z + d, 8) + xl))
        return 0

    lax.fori_loop(1, 8, greet, 0)

    col8 = jnp.zeros((8, B), F32)
    for k in range(NC):
        cnt_copy(k).wait()

        def strip(i, acc, k=k):
            x = cnt[rows(k * (C // 8) + i, 8), :].astype(F32)
            p = x[:, 0:128]
            for q in range(1, 8):
                p = p + x[:, q * 128 : (q + 1) * 128]
            part[rows(i, 8), :] = p
            return acc + x

        col8 = lax.fori_loop(0, C // 8, strip, col8, unroll=4)
        rs_mine[k : k + 1, :] = jnp.sum(part[...].T, axis=0, keepdims=True)
    col1 = jnp.sum(col8, axis=0, keepdims=True)
    for k in range(8):
        cs_mine[k : k + 1, :] = col1[:, k * 128 : (k + 1) * 128]

    vec_in.wait()
    pl.semaphore_wait(barrier, 38)

    pair_row = remote(rs_mine, rs_got, pair_s.at[0], pair_r.at[0], (r, c_other))
    pair_col = remote(cs_mine, cs_got, pair_s.at[1], pair_r.at[1], (r_other, c))
    pair_tot = remote(tot_mine, tot_got, pair_s.at[2], pair_r.at[2], (r_other, c))

    pair_row.start()
    pair_col.start()

    def zr_copy(i, slot):
        return remote(vec_ref, zrow.at[slot], zr_s.at[i], zr_r.at[slot], (r, 2 * i + xl))

    def zr_start(d, _):
        i = lax.rem(d + m - z + 8, 8)

        @pl.when(i != z)
        def _():
            zr_copy(i, z).start()

        return 0

    def rv_copy(i, half):
        return remote(
            zrow.at[i], rowv.at[rows(r, S)], rv_s.at[2 * i + half], rv_r.at[r], (2 * i + xl, 2 * z + half)
        )

    def rv_keeps(i, half):
        return jnp.logical_and(2 * i + xl == r, half == xl)

    def rv_send(i):
        for half in range(2):

            @pl.when(jnp.logical_not(rv_keeps(i, half)))
            def _():
                rv_copy(i, half).start()

            @pl.when(rv_keeps(i, half))
            def _():
                rowv[rows(r, S), :] = zrow[i]

    def rv_forward(p):
        i = lax.rem(p + m - z + 8, 8)

        @pl.when(i != z)
        def _():
            zr_copy(i, i).wait_recv()
            rv_send(i)

    lax.fori_loop(0, 8, zr_start, 0)
    zrow[z] = vec_ref[...]
    rv_send(z)

    def cv_copy(d):
        return remote(
            vec_ref, colv.at[rows(r, S)], cv_s.at[d], cv_r.at[r], (2 * lax.rem(m + d, 8) + core, c)
        )

    cv_core = remote(vec_ref, colv.at[rows(r, S)], cv_s.at[0], cv_r.at[r], (r_other, c))
    for d in range(1, 8):
        cv_copy(d).start()
    cv_core.start()
    colv[rows(r, S), :] = vec_ref[...]

    def cf_copy(d):
        o = 2 * lax.rem(m + d, 8) + core
        block = colv.at[rows(o, S)]
        return remote(block, block, cf_s.at[d], cv_r.at[o], (r_other, c))

    def cv_forward(d):
        cf_copy(d).wait_recv()
        cf_copy(d).start()

    def tile_copy(axis, src, dst, ssem, rsem, o, slot):
        dev = (2 * o + core, c) if axis == 0 else (r, 2 * o + xl)
        return remote(src, dst.at[slot], ssem.at[o], rsem.at[slot], dev)

    def spread(axis, src, dst, ssem, rsem):
        me = m if axis == 0 else z

        def one(d, _):
            tile_copy(axis, src, dst, ssem, rsem, lax.rem(me + d, 8), me).start()
            return 0

        lax.fori_loop(1, 8, one, 0)
        dst[me] = src[...]

    def collect(axis, src, dst, ssem, rsem):
        me = m if axis == 0 else z

        def one(d, _):
            o = lax.rem(me + d, 8)
            tile_copy(axis, src, dst, ssem, rsem, o, o).wait()
            return 0

        lax.fori_loop(1, 8, one, 0)
        return jnp.sum(dst[...], axis=0)

    rm = (1, rs_two, rs_all, rm_s, rm_r)
    cm = (0, cs_two, cs_all, cm_s, cm_r)
    tm = (0, tot_two, tot_all, tm_s, tm_r)

    def prep(i, _):
        x = cnt[rows(i, 8), :].astype(F32)
        logx[rows(i, 8), :] = jnp.log(jnp.maximum(x, 1.0))
        w = (1.0 / 32.0) * (0.1 + 0.25 * jnp.sqrt(x))
        weight[rows(i, 8), :] = jnp.where(x > 0.0, w, 0.0)
        return 0

    def prep_part(k):
        lax.fori_loop(k * 32, (k + 1) * 32, prep, 0, unroll=2)

    for k in range(4):
        prep_part(k)
    pair_row.wait()
    rs_two[...] = rs_mine[...] + rs_got[...]
    spread(*rm)
    pair_col.wait()
    cs_two[...] = cs_mine[...] + cs_got[...]
    spread(*cm)
    rv_forward(0)
    cv_forward(1)
    rv_forward(1)
    cv_forward(2)
    cv_forward(3)
    rv_forward(2)
    cv_forward(4)
    cv_forward(5)
    rsum = collect(*rm)
    tot_mine[...] = jnp.full((8, 128), jnp.sum(rsum), F32)
    pair_tot.start()
    rv_forward(3)
    cv_forward(6)
    cv_forward(7)
    pair_tot.wait()
    tot_two[...] = tot_mine[...] + tot_got[...]
    spread(*tm)
    rv_forward(4)
    rv_forward(5)
    rlog = jnp.log(rsum)
    for k in range(NC):
        rt[k * C : (k + 1) * C, :] = jnp.broadcast_to(rlog[k : k + 1, :], (C, 128)).T
    clog = jnp.log(collect(*cm))
    cv_core.wait_send()

    def cv_rest(d, _):
        o = 2 * lax.rem(m + d, 8) + 1 - core
        block = colv.at[rows(o, S)]
        remote(block, block, cf_s.at[0], cv_r.at[o], (r_other, c)).wait_recv()
        return 0

    lax.fori_loop(0, 8, cv_rest, 0)
    clog = clog - jnp.log(collect(*tm))
    for k in range(8):
        ct[0:1, k * 128 : (k + 1) * 128] = clog[k : k + 1, :]

    def md_copy(j):
        return remote(rsend.at[rows(j, S)], mid.at[2 * m + xl], md_s.at[j], md_r.at[2 * m + xl], (j, 2 * z + core))

    def chunk(p):
        n = near(p)
        here = rows(n, C)
        for half in range(2):
            j = 2 * n + half
            block = rowv.at[rows(j, S)]

            @pl.when(jnp.logical_not(jnp.logical_and(stays, j == r)))
            def _():
                remote(block, block, rv_s.at[j], rv_r.at[j], (r_other, c)).wait_recv()

        score[...] = lax.dot_general(
            rowv[here, :], colv[...], (((1,), (1,)), ((), ())), preferred_element_type=F32
        )

        def strip(i, _):
            at = rows(n * (C // 16) + i, 16)
            rl = rt[at, :]
            rl = jnp.concatenate([rl] * 8, axis=1)
            gap = score[rows(i, 16), :] - logx[at, :] + (rl + ct[0:1, :])
            w = weight[at, :]
            sig = (1.0 / 64.0) + (1.0 / 64.0) * jnp.tanh(0.5 * gap)
            resid[at, :] = jnp.where(w > 0.0, w * gap, sig).astype(BF16)
            return 0

        lax.fori_loop(0, C // 16, strip, 0, unroll=4)
        out = jnp.dot(resid[here, :], colv[...], preferred_element_type=F32)

        rsend[here, :] = out.astype(BF16)
        for half in range(2):
            mine = jnp.logical_and(stays, 2 * n + half == r)

            @pl.when(jnp.logical_not(mine))
            def _():
                md_copy(2 * n + half).start()

            @pl.when(mine)
            def _():
                mid[2 * m + xl] = rsend[rows(2 * n + half, S), :]

    def rg_copy(n, slot):
        return remote(zsend.at[n], rrecv.at[slot], rg_s.at[n], rg_r.at[slot], (r, 2 * n + xl))

    def reduce(p):
        n = lax.rem(m - z + p + 8, 8)
        for half in range(2):
            slot = 2 * n + half

            @pl.when(jnp.logical_not(jnp.logical_and(stays, slot == 2 * m + xl)))
            def _():
                remote(mid.at[slot], mid.at[slot], md_s.at[0], md_r.at[slot], (r_other, c)).wait_recv()

        zsend[n] = (mid[2 * n].astype(F32) + mid[2 * n + 1].astype(F32)).astype(BF16)

        @pl.when(n != z)
        def _():
            rg_copy(n, z).start()

        @pl.when(n == z)
        def _():
            rrecv[z] = zsend[n]

    def cx_copy(n):
        return remote(cxs.at[n], cxr.at[n], cx_s.at[n], cx_r.at[n], (r_other, c))

    def col_pair(d, _):
        q = lax.rem(m // 2 + d, 4)
        out = lax.dot_general(
            resid[:, rows(q, 2 * C)], rowv[...], (((0,), (0,)), ((), ())), preferred_element_type=F32
        )
        for k in range(2):
            n = 2 * q + k
            low, high = out[k * C : k * C + S], out[k * C + S : (k + 1) * C]

            @pl.when(core == 0)
            def _():
                cown[n] = low
                cxs[n] = high.astype(BF16)

            @pl.when(core == 1)
            def _():
                cown[n] = high
                cxs[n] = low.astype(BF16)

            cx_copy(n).start()
        return 0

    def cg_copy(n, slot):
        return remote(csend.at[n], crecv.at[slot], cg_s.at[n], cg_r.at[slot], (2 * n + core, c))

    def col_sum(d, _):
        n = lax.rem(m + d, 8)
        cx_copy(n).wait_recv()
        csend[n] = (cown[n] + cxr[n].astype(F32)).astype(BF16)
        cg_copy(n, m).start()
        return 0

    LAG = 6

    def forward_loop(p, _):
        @pl.when(p < 2)
        def _():
            rv_forward(p + 6)

        chunk(p)

        @pl.when(p >= LAG)
        def _():
            reduce(p - LAG)

        return 0

    lax.fori_loop(0, NC, forward_loop, 0)
    def reduce_loop(p, _):
        reduce(p)
        return 0

    lax.fori_loop(1, 3, col_pair, 0)
    lax.fori_loop(NC - LAG, NC - 3, reduce_loop, 0)
    lax.fori_loop(3, 5, col_pair, 0)
    lax.fori_loop(1, 8, col_sum, 0)
    lax.fori_loop(NC - 3, NC, reduce_loop, 0)
    cx_copy(m).wait_recv()
    grad = cown[m] + cxr[m].astype(F32)

    def col_recv(d, acc):
        n = lax.rem(m + d, 8)
        cg_copy(n, n).wait_recv()
        return acc + crecv[n].astype(F32)

    grad = lax.fori_loop(1, 8, col_recv, grad)

    def row_recv(d, acc):
        i = lax.rem(z + d, 8)

        @pl.when(i != z)
        def _():
            rg_copy(i, i).wait_recv()

        return acc + rrecv[i].astype(F32)

    grad = lax.fori_loop(0, 8, row_recv, grad)
    grad_ref[...] = grad

    def sent(i, _):
        @pl.when(i != z)
        def _():
            zr_copy(i, z).wait_send()
            rg_copy(i, z).wait_send()

        cx_copy(i).wait_send()
        for half in range(2):

            @pl.when(jnp.logical_not(rv_keeps(i, half)))
            def _():
                rv_copy(i, half).wait_send()

            @pl.when(jnp.logical_not(jnp.logical_and(stays, 2 * i + half == r)))
            def _():
                md_copy(2 * i + half).wait_send()

        @pl.when(i != m)
        def _():
            cg_copy(i, m).wait_send()

        @pl.when(i != 0)
        def _():
            cv_copy(i).wait_send()
            cf_copy(i).wait_send()

        return 0

    lax.fori_loop(0, 8, sent, 0)


def shards(counts, vectors, accum):
    vmem = pl.BlockSpec(memory_space=pltpu.VMEM)
    hbm = pl.BlockSpec(memory_space=pltpu.HBM)
    dma = pltpu.SemaphoreType.DMA
    many = dma((N,))
    eight = dma((8,))
    three = dma((3,))
    tile = pltpu.VMEM((8, 128), F32)
    tiles = pltpu.VMEM((8, 8, 128), F32)
    half = pltpu.VMEM((8, S, D), BF16)
    grad = pl.pallas_call(
        kernel,
        out_shape=jax.ShapeDtypeStruct((S, D), F32),
        in_specs=[hbm, hbm],
        out_specs=vmem,
        scratch_shapes=[
            pltpu.VMEM((S, D), BF16),
            pltpu.VMEM((B, B), jnp.int32),
            pltpu.VMEM((B, D), BF16),
            half,
            pltpu.VMEM((B, D), BF16),
            pltpu.VMEM((B, B), F32),
            pltpu.VMEM((B, B), F32),
            pltpu.VMEM((B, B), BF16),
            pltpu.VMEM((C, B), F32),
            pltpu.VMEM((C, 128), F32),
            pltpu.VMEM((8, B), F32),
            pltpu.VMEM((B, 128), F32),
            tile, tile, tile, tile, tile, tile, tile, tile, tile, tiles, tiles, tiles,
            pltpu.VMEM((B, D), BF16), pltpu.VMEM((N, S, D), BF16), half, half,
            pltpu.VMEM((8, S, D), F32), half, half, half, half,
            dma(()), eight, eight, many, eight, eight, eight, many, many,
            three, three, eight, eight, eight, eight, eight, eight,
            many, many, eight, eight, eight, eight, eight, eight,
        ],
        compiler_params=pltpu.CompilerParams(
            collective_id=1, has_side_effects=True, vmem_limit_bytes=50 * 2**20
        ),
        name="swivel_step",
    )(counts, vectors)
    accum_new = accum + grad * grad
    updated = (vectors.astype(F32) - 0.5 * grad / jnp.sqrt(accum_new)).astype(BF16)
    return updated, accum_new


def solution(mesh):
    return jax.shard_map(
        shards,
        mesh=mesh,
        in_specs=(P("row", "col"), P(("col", "row"), None), P(("col", "row"), None)),
        out_specs=(P(("col", "row"), None), P(("col", "row"), None)),
        check_vma=False,
    )
```
